32 devices in a mesh: tile: 16 (over z, y, core), pair: 2 (over x).
Axes of the slice: x: 2, y: 2, z: 4, core: 2. Of those that a mesh axis runs over, the one named last changes fastest.
Arguments:
- state: bfloat16 [2, 32, 256, 512], P('pair', None, 'tile'), may hold values from -6 to 6
- target: bfloat16 [2, 32, 256, 512], P('pair', None, 'tile'), may hold values from -6 to 6
- perturbation: bfloat16 [2, 32, 256, 512], P('pair', None, 'tile'), may hold values from -4 to 4
- legendre: bfloat16 [256, 256, 256], P('tile'), may hold values from -0.375 to 0.375
- damp: float32 [32, 256], replicated, may hold values from 0.3 to 3
Outputs:
- grad_state: float32 [2, 32, 256, 512], P('pair', None, 'tile')
- grad_damp: float32 [32, 256], replicated
The draws below stay inside these ranges and needn't reach their ends.
All inputs are finite; a program needn't handle non-finite values.
Results may differ from the reference program's by a relative error of at most 0.007.
Values may be sent and summed in bfloat16 or wider, within the bound.
A program may use at most 64 MiB of HBM per device.

```python
import math
import jax
import jax.numpy as jnp
from jax import lax

NLON = 512
NLAT = 256
M = 256
NT = 256
LEV = 32
MEM = 2
N_PAIR = 2


def block_scale(key, dims, split, least, top_value):
    level, own = 1.0, jax.random.fold_in(key, 6)
    for dim, parts in split:
        draws = jnp.exp(jax.random.uniform(jax.random.fold_in(own, dim), (parts,), jnp.float32, least / len(split), top_value / len(split)))
        level = level * jnp.repeat(draws, dims[dim] // parts).reshape([-1 if axis == dim else 1 for axis in range(len(dims))])
    return level


def bell_draw(own_key, extent, scale, bound, shards=(), kind=jnp.bfloat16):
    array = scale * jax.random.normal(own_key, extent, jnp.float32)
    if shards:
        array = array * block_scale(own_key, extent, shards, -0.22, 0.18)
    return jnp.clip(array, -bound, bound).astype(kind)


def setup_inputs(seed: int = 0) -> dict:
    streams_of = jax.random.split(jax.random.key(seed), 6)
    return {
        "state": bell_draw(streams_of[0], (MEM, LEV, NLAT, NLON), 1.0, 6.0, ((0, 2), (2, 16))),
        "target": bell_draw(streams_of[1], (MEM, LEV, NLAT, NLON), 1.0, 6.0, ((0, 2), (2, 16))),
        "perturbation": bell_draw(streams_of[2], (MEM, LEV, NLAT, NLON), 0.5, 4.0, ((0, 2), (2, 16))),
        "legendre": bell_draw(streams_of[3], (M, NT, NLAT), NLAT ** -0.5, 0.375, ((0, 16),)),
        "damp": jnp.clip(jnp.exp(jax.random.uniform(streams_of[4], (LEV, NT), jnp.float32, math.log(0.3), math.log(3.0))), 0.3, 3.0),
    }


HIGH = lax.Precision.HIGHEST

def fourier_table(length, waves):
    points = jnp.arange(length, dtype=jnp.int32)
    orders = jnp.arange(waves, dtype=jnp.int32)
    phase = points[:, None] * orders[None, :] % length
    angle = phase.astype(jnp.float32) * (2.0 * math.pi / length)
    stacked = jnp.stack([jnp.cos(angle), -jnp.sin(angle)], axis=1)
    return (stacked * length ** (-0.5)).astype(jnp.bfloat16)

def rounded(value):
    return lax.optimization_barrier(value.astype(jnp.bfloat16)).astype(jnp.float32)

def reference(state, target, perturbation, legendre, damp):
    table = fourier_table(NLON, M).astype(jnp.float32)
    wave_ids = jnp.arange(M, dtype=jnp.int32)
    degree = jnp.arange(NT, dtype=jnp.int32)
    masked = jnp.where(degree[None, :, None] >= wave_ids[:, None, None], legendre, jnp.zeros_like(legendre)).astype(jnp.float32)
    gain = damp[:, None, None, :]

    def analyse(grid):
        return rounded(jnp.einsum('lgj,jrm->lrmg', grid, table, precision=HIGH))

    def synthesise(spec):
        return jnp.einsum('lrmg,jrm->lgj', spec, table, precision=HIGH)

    def spectral(grid_coef):
        coef = jnp.einsum('lrmg,mng->lrmn', grid_coef, masked, precision=HIGH)
        filtered = rounded(coef * gain)
        back = rounded(jnp.einsum('lrmn,mng->lrmg', filtered, masked, precision=HIGH))
        return (back, coef)

    def forward(field, noise):
        start = field.astype(jnp.float32)
        back, coef = spectral(analyse(start))
        bent = jnp.tanh(synthesise(back))
        advanced = rounded(start + bent + noise.astype(jnp.float32))
        return (advanced, bent, coef)

    def first_pass(items):
        return forward(items[0], items[1])[0].astype(jnp.bfloat16)
    advanced_all = lax.map(first_pass, (state, perturbation))
    count = advanced_all.shape[0]
    grouped = advanced_all.reshape(N_PAIR // 2, 2, count // N_PAIR, LEV, NLAT, NLON)
    partner_all = grouped[:, ::-1].reshape(count, LEV, NLAT, NLON)

    def second_pass(items):
        field, noise, truth, other = items
        advanced, bent, coef = forward(field, noise)
        miss = advanced - truth.astype(jnp.float32)
        spread = advanced - other.astype(jnp.float32)
        grad_adv = 0.5 * miss * lax.rsqrt(miss * miss + 1.0) - 0.25 * spread * lax.rsqrt(spread * spread + 1.0)
        grad_wave = rounded(grad_adv * (1.0 - bent * bent))
        grad_fourier, grad_coef = spectral(analyse(grad_wave))
        grad_state = grad_adv + synthesise(grad_fourier)
        partial_sum = lax.optimization_barrier(jnp.sum(coef * grad_coef, axis=(1, 2)))
        return (grad_state, partial_sum)
    grads, partials = lax.map(second_pass, (state, perturbation, target, partner_all))
    grad_damp = lax.optimization_barrier(jnp.sum(partials, axis=0)) * (MEM * M) ** (-0.5)
    return (grads, grad_damp)
```

```python
import functools
import math

import jax
import jax.numpy as jnp
import ml_dtypes
import numpy as np
from jax import lax
from jax.experimental import pallas as pl
from jax.experimental.pallas import tpu as pltpu
from jax.sharding import PartitionSpec as P

NLON = 512
M = 256


def swapped(value, axis, distance):
    mask = 2**distance
    pairs = [(source, source ^ mask) for source in range(lax.axis_size(axis))]
    return lax.ppermute(value, axis, pairs)


def fourier_table(length, waves):
    points = jnp.arange(length, dtype=jnp.int32)
    orders = jnp.arange(waves, dtype=jnp.int32)
    phase = points[:, None] * orders[None, :] % length
    angle = phase.astype(jnp.float32) * (2.0 * math.pi / length)
    stacked = jnp.stack([jnp.cos(angle), -jnp.sin(angle)], axis=1)
    return (stacked * length ** (-0.5)).astype(jnp.bfloat16)


def body(state, target, perturbation, legendre, damp):
    table = fourier_table(NLON, M)
    waves_dev = legendre.shape[0]
    first = lax.axis_index("tile") * waves_dev
    wave_ids = first + jnp.arange(waves_dev, dtype=jnp.int32)
    degree = jnp.arange(legendre.shape[1], dtype=jnp.int32)
    masked = jnp.where(
        degree[None, :, None] >= wave_ids[:, None, None], legendre, jnp.zeros_like(legendre)
    )
    gain = damp[None, :, None, None, :]

    def analyse(grid):
        return jnp.einsum(
            "blgj,jrm->blrmg", grid, table, preferred_element_type=jnp.float32
        ).astype(jnp.bfloat16)

    def synthesise(spec):
        return jnp.einsum("blrmg,jrm->blgj", spec, table, preferred_element_type=jnp.float32)

    def spectral_pass(piece, sender):
        coef = jnp.einsum("blrmg,mng->blrmn", piece, masked, preferred_element_type=jnp.float32)
        filtered = (coef * gain).astype(jnp.bfloat16)
        back = jnp.einsum(
            "blrmn,mng->blrmg", filtered, masked, preferred_element_type=jnp.float32
        ).astype(jnp.bfloat16)
        return (sender(back), coef)

    def to_grid(back):
        return lax.all_to_all(back, "tile", split_axis=4, concat_axis=3, tiled=True)

    def spectral(grid_coef):
        spec = lax.all_to_all(grid_coef, "tile", split_axis=3, concat_axis=4, tiled=True)
        return spectral_pass(spec, to_grid)

    back_grid, coef = spectral(analyse(state))
    bent = jnp.tanh(synthesise(back_grid))
    advanced = (state.astype(jnp.float32) + bent + perturbation.astype(jnp.float32)).astype(
        jnp.bfloat16
    )
    partner = swapped(advanced, "pair", 0)
    mine = advanced.astype(jnp.float32)
    miss = mine - target.astype(jnp.float32)
    spread = mine - partner.astype(jnp.float32)
    grad_adv = 0.5 * miss * lax.rsqrt(miss * miss + 1.0) - 0.25 * spread * lax.rsqrt(
        spread * spread + 1.0
    )
    grad_wave = (grad_adv * (1.0 - bent * bent)).astype(jnp.bfloat16)
    grad_fourier, grad_coef = spectral(analyse(grad_wave))
    grad_state = grad_adv + synthesise(grad_fourier)
    partial_sum = jnp.sum(coef * grad_coef, axis=(0, 2, 3))
    total = lax.psum(partial_sum, ("tile", "pair"))
    members = state.shape[0] * lax.axis_size("pair")
    return (grad_state, total * (members * M) ** (-0.5))


MESH = pl.DeviceIdType.MESH
BF16, F32 = jnp.bfloat16, jnp.float32
SIDE = 16
CHUNKS = 2


def table_rows(length, waves):
    points = np.arange(length)
    orders = np.arange(waves)
    angle = (points[:, None] * orders[None, :] % length) * (2.0 * math.pi / length)
    both = np.stack([np.cos(angle), -np.sin(angle)], axis=0) * length ** (-0.5)
    split = both.reshape(2, length, waves // SIDE, 2, 8)
    return split.transpose(4, 0, 2, 3, 1).reshape(2 * waves, length).astype(ml_dtypes.bfloat16)


def exchanged(parts):
    lane = lax.broadcasted_iota(jnp.int32, parts[0].shape, 1)
    parts = list(parts)
    for bit in (1, 2, 4, 8):
        high = (lane & bit) != 0
        for i in range(16):
            if not i & bit:
                a, b = parts[i], parts[i | bit]
                parts[i] = jnp.where(high, pltpu.roll(b, bit, 1), a)
                parts[i | bit] = jnp.where(high, b, pltpu.roll(a, 128 - bit, 1))
    return parts


def kernel(
    tiles, pairs, levels,
    state, table, damp, target_hbm, pert_hbm, leg_hbm,
    out, total,
    target, pert, leg, mk_n, mk_g, rhs, gain, coefs, dacc, bents, adv, other, gw, wave,
    four, turned, send, recv, rs_src, rs_recv, ag_src, ag_recv,
    load_sem, send_sem, recv_sem, psend_sem, precv_sem, rs_sem, ag_sem,
):
    me, mine = lax.axis_index("tile"), lax.axis_index("pair")
    flat = mine * tiles + me
    count = tiles * pairs
    lev = levels // CHUNKS
    blocks = lev // 8
    rows = lev * SIDE
    width = blocks * 128
    buddy = mine + 1 - 2 * lax.rem(mine, 2)

    loads = [
        pltpu.make_async_copy(src, dst, load_sem.at[i])
        for i, (src, dst) in enumerate(((leg_hbm, leg), (pert_hbm, pert), (target_hbm, target)))
    ]
    for load in loads:
        load.start()

    barrier = pltpu.get_barrier_semaphore()

    def greet(step, _):
        to = lax.rem(flat + step, count)
        pl.semaphore_signal(
            barrier, inc=1,
            device_id={"tile": lax.rem(to, tiles), "pair": to // tiles}, device_id_type=MESH,
        )
        return 0

    lax.fori_loop(1, count, greet, 0)

    def all_to_all(slot):
        def one(step, _):
            to = lax.rem(me + step, tiles)
            pltpu.make_async_remote_copy(
                src_ref=send.at[slot, to], dst_ref=recv.at[slot, me],
                send_sem=send_sem.at[slot], recv_sem=recv_sem.at[slot],
                device_id={"tile": to}, device_id_type=MESH,
            ).start()
            return 0

        lax.fori_loop(1, tiles, one, 0)
        pltpu.make_async_copy(send.at[slot, me], recv.at[slot, me], recv_sem.at[slot]).start()

    def arrived(slot):
        pltpu.make_async_copy(recv.at[slot], recv.at[slot], recv_sem.at[slot]).wait()

    def analyse(slot, grid):
        four[...] = lax.dot_general(
            table[...], grid, (((1,), (1,)), ((), ())), preferred_element_type=F32
        )
        for b in range(blocks):
            lanes = pl.ds(b * 128, 128)

            def turn(ro, _):
                at = pl.multiple_of(ro * 8, 8)
                parts = exchanged([four[pl.ds(c * 32 + at, 8), lanes] for c in range(16)])
                for g in range(16):
                    turned[pl.ds(g * 32 + at, 8), :] = parts[g]
                return 0

            lax.fori_loop(0, 4, turn, 0)
            for row in range(32):
                send[slot, row // 2, (row % 2) * blocks + b] = turned[
                    pl.ds(row, 16, stride=32), :
                ].astype(BF16)

    def synthesise(slot):
        for b in range(blocks):
            lanes = pl.ds(b * 128, 128)
            for row in range(32):
                turned[pl.ds(row * 16, 16), :] = recv[
                    slot, row // 2, (row % 2) * blocks + b
                ].astype(F32)

            def turn(ro, _):
                at = pl.multiple_of(ro * 8, 8)
                parts = exchanged(
                    [turned[pl.ds(at * 16 + g, 8, stride=16), :] for g in range(16)]
                )
                for c in range(16):
                    four[pl.ds(c * 32 + at, 8), lanes] = parts[c]
                return 0

            lax.fori_loop(0, 4, turn, 0)
        wave[...] = lax.dot_general(
            four[...].astype(BF16), table[...], (((0,), (0,)), ((), ())),
            preferred_element_type=F32,
        )

    lane_m = lax.rem(lax.broadcasted_iota(jnp.int32, (SIDE * 16, width), 1), 16) // 2

    def spread(value):
        for m in range(8):
            rhs[pl.ds(m * 256, 256), :] = jnp.where(lane_m == m, value, 0.0).astype(BF16)

    def spectral(ch, slot_in, slot_out, backward):
        for hi in range(2):
            held = [
                recv[slot_in, :, hi * blocks + b].reshape(SIDE * SIDE, 128).astype(F32)
                for b in range(blocks)
            ]
            spread(jnp.concatenate(held, axis=1))
            coef = jnp.dot(mk_n[hi], rhs[...], preferred_element_type=F32)
            if backward:
                product = coefs[ch, hi] * coef
                dacc[ch] = product if hi == 0 else dacc[ch] + product
            else:
                coefs[ch, hi] = coef
            spread(coef * gain[ch])
            back = jnp.dot(mk_g[hi], rhs[...], preferred_element_type=F32).astype(BF16)
            for b in range(blocks):
                send[slot_out, :, hi * blocks + b] = back[:, b * 128 : b * 128 + 128].reshape(
                    SIDE, SIDE, 128
                )

    def pick(ch):
        level = lax.broadcasted_iota(jnp.int32, (levels, width), 0)
        lane = lax.broadcasted_iota(jnp.int32, (levels, width), 1)
        return (level == ch * lev + lane // 16).astype(F32)

    def exchange(ch):
        return pltpu.make_async_remote_copy(
            src_ref=adv.at[ch], dst_ref=other.at[ch],
            send_sem=psend_sem.at[ch], recv_sem=precv_sem.at[ch],
            device_id={"pair": buddy}, device_id_type=MESH,
        )

    for ch in range(CHUNKS):
        analyse(ch, state[pl.ds(ch * rows, rows), :])
        if ch == 0:
            pl.semaphore_wait(barrier, count - 1)
        all_to_all(ch)

    loads[0].wait()
    for i in range(16):
        degree = lax.broadcasted_iota(jnp.int32, (256, 256), 0)
        own = jnp.where(degree >= me * SIDE + i, leg[i].astype(F32), 0.0)
        at = pl.ds((i % 8) * 256, 256)
        mk_n[i // 8, :, at] = own.astype(BF16)
        mk_g[i // 8, :, at] = own.T.astype(BF16)
    for ch in range(CHUNKS):
        gain[ch] = lax.dot_general(
            damp[...], pick(ch), (((0,), (0,)), ((), ())),
            precision=lax.Precision.HIGHEST, preferred_element_type=F32,
        )
    loads[1].wait()
    loads[2].wait()

    for ch in range(CHUNKS):
        arrived(ch)
        spectral(ch, ch, CHUNKS + ch, False)
        all_to_all(CHUNKS + ch)

    for ch in range(CHUNKS):
        arrived(CHUNKS + ch)
        synthesise(CHUNKS + ch)

        def advance(step, _):
            at = pl.ds(pl.multiple_of(step * 16, 16), 16)
            all_at = pl.ds(pl.multiple_of(ch * rows + step * 16, 16), 16)
            bent = jnp.tanh(wave[at, :])
            bents[all_at, :] = bent
            adv[ch, at, :] = (
                state[all_at, :].astype(F32) + bent + pert[all_at, :].astype(F32)
            ).astype(BF16)
            return 0

        lax.fori_loop(0, rows // 16, advance, 0)
        exchange(ch).start()

    for ch in range(CHUNKS):
        exchange(ch).wait_recv()

        def gradient(step, _):
            at = pl.ds(pl.multiple_of(step * 16, 16), 16)
            all_at = pl.ds(pl.multiple_of(ch * rows + step * 16, 16), 16)
            own = adv[ch, at, :].astype(F32)
            miss = own - target[all_at, :].astype(F32)
            apart = own - other[ch, at, :].astype(F32)
            grad_adv = 0.5 * miss * lax.rsqrt(miss * miss + 1.0) - 0.25 * apart * lax.rsqrt(
                apart * apart + 1.0
            )
            bent = bents[all_at, :]
            out[all_at, :] = grad_adv
            gw[at, :] = (grad_adv * (1.0 - bent * bent)).astype(BF16)
            return 0

        lax.fori_loop(0, rows // 16, gradient, 0)
        analyse(2 * CHUNKS + ch, gw[...])
        all_to_all(2 * CHUNKS + ch)

    for ch in range(CHUNKS):
        arrived(2 * CHUNKS + ch)
        spectral(ch, 2 * CHUNKS + ch, 3 * CHUNKS + ch, True)
        all_to_all(3 * CHUNKS + ch)

    partial = sum(
        lax.dot_general(
            pick(ch), dacc[ch], (((1,), (1,)), ((), ())),
            precision=lax.Precision.HIGHEST, preferred_element_type=F32,
        )
        for ch in range(CHUNKS)
    )
    owners = levels // 8 * 2
    for k in range(owners):
        rs_src[k] = partial[k // 2 * 8 : k // 2 * 8 + 8, k % 2 * 128 : k % 2 * 128 + 128]

    def rs_copy(k):
        return pltpu.make_async_remote_copy(
            src_ref=rs_src.at[k], dst_ref=rs_recv.at[flat],
            send_sem=rs_sem.at[1 + k], recv_sem=rs_sem.at[0],
            device_id={"tile": 2 * k, "pair": k % pairs}, device_id_type=MESH,
        )

    for k in range(owners):
        is_owner = flat == (k % pairs) * tiles + 2 * k

        @pl.when(jnp.logical_not(is_owner))
        def _():
            rs_copy(k).start()

        @pl.when(is_owner)
        def _():
            pltpu.make_async_copy(rs_src.at[k], rs_recv.at[flat], rs_sem.at[0]).start()

    block = me // 2
    owns = jnp.logical_and(lax.rem(me, 2) == 0, lax.rem(block, pairs) == mine)

    @pl.when(owns)
    def _():
        pltpu.make_async_copy(rs_recv, rs_recv, rs_sem.at[0]).wait()
        ag_src[...] = jnp.sum(rs_recv[...], axis=0)

        def one(step, _):
            to = lax.rem(flat + step, count)
            pltpu.make_async_remote_copy(
                src_ref=ag_src, dst_ref=ag_recv.at[block],
                send_sem=ag_sem.at[1], recv_sem=ag_sem.at[0],
                device_id={"tile": lax.rem(to, tiles), "pair": to // tiles}, device_id_type=MESH,
            ).start()
            return 0

        lax.fori_loop(1, count, one, 0)
        pltpu.make_async_copy(ag_src, ag_recv.at[block], ag_sem.at[0]).start()

    for ch in range(CHUNKS):
        arrived(3 * CHUNKS + ch)
        synthesise(3 * CHUNKS + ch)
        at = pl.ds(ch * rows, rows)
        out[at, :] = out[at, :] + wave[...]

    pltpu.make_async_copy(ag_recv, ag_recv, ag_sem.at[0]).wait()
    for k in range(owners):
        total[k // 2 * 8 : k // 2 * 8 + 8, k % 2 * 128 : k % 2 * 128 + 128] = ag_recv[k] * (
            (pairs * tiles * SIDE) ** (-0.5)
        )

    for slot in range(4 * CHUNKS):
        gone = send.at[slot, pl.ds(0, tiles - 1)]
        pltpu.make_async_copy(gone, gone, send_sem.at[slot]).wait()
    for ch in range(CHUNKS):
        exchange(ch).wait_send()
    for k in range(owners):
        @pl.when(flat != (k % pairs) * tiles + 2 * k)
        def _():
            rs_copy(k).wait_send()

    @pl.when(owns)
    def _():
        gone = rs_recv.at[pl.ds(0, count - 1)]
        pltpu.make_async_copy(gone, gone, ag_sem.at[1]).wait()


def fused(tiles, pairs, state, target, perturbation, legendre, damp):
    members, levels, lats, lons = state.shape
    rows = levels * lats
    part = rows // CHUNKS
    width = levels // CHUNKS // 8 * 128
    blocks = width // 128 * 2
    flatten = lambda x: x.reshape(rows, lons)
    dma = pltpu.SemaphoreType.DMA
    grads, total = pl.pallas_call(
        functools.partial(kernel, tiles, pairs, levels),
        out_shape=(
            jax.ShapeDtypeStruct((rows, lons), F32),
            jax.ShapeDtypeStruct(damp.shape, F32),
        ),
        in_specs=[pl.BlockSpec(memory_space=pltpu.VMEM)] * 3
        + [pl.BlockSpec(memory_space=pl.ANY)] * 3,
        out_specs=(pl.BlockSpec(memory_space=pltpu.VMEM),) * 2,
        scratch_shapes=[
            pltpu.VMEM((rows, lons), BF16),
            pltpu.VMEM((rows, lons), BF16),
            pltpu.VMEM(legendre.shape, BF16),
            pltpu.VMEM((2, 256, 2048), BF16),
            pltpu.VMEM((2, 256, 2048), BF16),
            pltpu.VMEM((2048, width), BF16),
            pltpu.VMEM((CHUNKS, 256, width), F32),
            pltpu.VMEM((CHUNKS, 2, 256, width), F32),
            pltpu.VMEM((CHUNKS, 256, width), F32),
            pltpu.VMEM((rows, lons), F32),
            pltpu.VMEM((CHUNKS, part, lons), BF16),
            pltpu.VMEM((CHUNKS, part, lons), BF16),
            pltpu.VMEM((part, lons), BF16),
            pltpu.VMEM((part, lons), F32),
            pltpu.VMEM((512, width), F32),
            pltpu.VMEM((512, 128), F32),
            pltpu.VMEM((4 * CHUNKS, tiles, blocks, SIDE, 128), BF16),
            pltpu.VMEM((4 * CHUNKS, tiles, blocks, SIDE, 128), BF16),
            pltpu.VMEM((8, 8, 128), F32),
            pltpu.VMEM((tiles * pairs, 8, 128), F32),
            pltpu.VMEM((8, 128), F32),
            pltpu.VMEM((8, 8, 128), F32),
            dma((3,)),
            dma((4 * CHUNKS,)),
            dma((4 * CHUNKS,)),
            dma((CHUNKS,)),
            dma((CHUNKS,)),
            dma((9,)),
            dma((2,)),
        ],
        compiler_params=pltpu.CompilerParams(
            collective_id=0, has_side_effects=True, vmem_limit_bytes=48 * 2**20
        ),
    )(
        flatten(state), jnp.asarray(table_rows(NLON, M)), damp,
        flatten(target), flatten(perturbation), legendre,
    )
    return grads.reshape(state.shape), total


def solution(mesh):
    placed = (
        P("pair", None, "tile", None),
        P("pair", None, "tile", None),
        P("pair", None, "tile", None),
        P("tile", None, None),
        P(),
    )
    tiles, pairs = mesh.shape["tile"], mesh.shape["pair"]

    def local(state, target, perturbation, legendre, damp):
        held = (state.shape, legendre.shape, damp.shape)
        small = ((1, 32, SIDE, NLON), (SIDE, 256, 256), (32, 256))
        if tiles == SIDE and pairs == 2 and held == small:
            return fused(tiles, pairs, state, target, perturbation, legendre, damp)
        return body(state, target, perturbation, legendre, damp)

    return jax.shard_map(
        local,
        mesh=mesh,
        in_specs=placed,
        out_specs=(P("pair", None, "tile", None), P()),
        check_vma=False,
    )
```

```python
import functools
import math

import jax
import jax.numpy as jnp
import ml_dtypes
import numpy as np
from jax import lax
from jax.experimental import pallas as pl
from jax.experimental.pallas import tpu as pltpu
from jax.sharding import PartitionSpec as P

NLON = 512
M = 256


def swapped(value, axis, distance):
    mask = 2**distance
    pairs = [(source, source ^ mask) for source in range(lax.axis_size(axis))]
    return lax.ppermute(value, axis, pairs)


def fourier_table(length, waves):
    points = jnp.arange(length, dtype=jnp.int32)
    orders = jnp.arange(waves, dtype=jnp.int32)
    phase = points[:, None] * orders[None, :] % length
    angle = phase.astype(jnp.float32) * (2.0 * math.pi / length)
    stacked = jnp.stack([jnp.cos(angle), -jnp.sin(angle)], axis=1)
    return (stacked * length ** (-0.5)).astype(jnp.bfloat16)


def body(state, target, perturbation, legendre, damp):
    table = fourier_table(NLON, M)
    waves_dev = legendre.shape[0]
    first = lax.axis_index("tile") * waves_dev
    wave_ids = first + jnp.arange(waves_dev, dtype=jnp.int32)
    degree = jnp.arange(legendre.shape[1], dtype=jnp.int32)
    masked = jnp.where(
        degree[None, :, None] >= wave_ids[:, None, None], legendre, jnp.zeros_like(legendre)
    )
    gain = damp[None, :, None, None, :]

    def analyse(grid):
        return jnp.einsum(
            "blgj,jrm->blrmg", grid, table, preferred_element_type=jnp.float32
        ).astype(jnp.bfloat16)

    def synthesise(spec):
        return jnp.einsum("blrmg,jrm->blgj", spec, table, preferred_element_type=jnp.float32)

    def spectral_pass(piece, sender):
        coef = jnp.einsum("blrmg,mng->blrmn", piece, masked, preferred_element_type=jnp.float32)
        filtered = (coef * gain).astype(jnp.bfloat16)
        back = jnp.einsum(
            "blrmn,mng->blrmg", filtered, masked, preferred_element_type=jnp.float32
        ).astype(jnp.bfloat16)
        return (sender(back), coef)

    def to_grid(back):
        return lax.all_to_all(back, "tile", split_axis=4, concat_axis=3, tiled=True)

    def spectral(grid_coef):
        spec = lax.all_to_all(grid_coef, "tile", split_axis=3, concat_axis=4, tiled=True)
        return spectral_pass(spec, to_grid)

    back_grid, coef = spectral(analyse(state))
    bent = jnp.tanh(synthesise(back_grid))
    advanced = (state.astype(jnp.float32) + bent + perturbation.astype(jnp.float32)).astype(
        jnp.bfloat16
    )
    partner = swapped(advanced, "pair", 0)
    mine = advanced.astype(jnp.float32)
    miss = mine - target.astype(jnp.float32)
    spread = mine - partner.astype(jnp.float32)
    grad_adv = 0.5 * miss * lax.rsqrt(miss * miss + 1.0) - 0.25 * spread * lax.rsqrt(
        spread * spread + 1.0
    )
    grad_wave = (grad_adv * (1.0 - bent * bent)).astype(jnp.bfloat16)
    grad_fourier, grad_coef = spectral(analyse(grad_wave))
    grad_state = grad_adv + synthesise(grad_fourier)
    partial_sum = jnp.sum(coef * grad_coef, axis=(0, 2, 3))
    total = lax.psum(partial_sum, ("tile", "pair"))
    members = state.shape[0] * lax.axis_size("pair")
    return (grad_state, total * (members * M) ** (-0.5))


MESH = pl.DeviceIdType.MESH
BF16, F32 = jnp.bfloat16, jnp.float32
SIDE = 16
BLOCKS = 4
STEP_OUT, STEP_IN = 40, 24


def table_rows(length, waves):
    points = np.arange(length)
    orders = np.arange(waves)
    angle = (points[:, None] * orders[None, :] % length) * (2.0 * math.pi / length)
    both = np.stack([np.cos(angle), -np.sin(angle)], axis=0) * length ** (-0.5)
    split = both.reshape(2, length, waves // SIDE, 2, 8)
    return split.transpose(4, 0, 2, 3, 1).reshape(2 * waves, length).astype(ml_dtypes.bfloat16)


def exchanged(parts):
    lane = lax.broadcasted_iota(jnp.int32, parts[0].shape, 1)
    parts = list(parts)
    for bit in (1, 2, 4, 8):
        high = (lane & bit) != 0
        for i in range(16):
            if not i & bit:
                a, b = parts[i], parts[i | bit]
                parts[i] = jnp.where(high, pltpu.roll(b, bit, 1), a)
                parts[i | bit] = jnp.where(high, b, pltpu.roll(a, 128 - bit, 1))
    return parts


def kernel(
    tiles, pairs, levels,
    state, table, damp, target_hbm, pert_hbm, leg_hbm,
    out, total,
    target, pert, leg, mk_n, mk_g, rhs, gain, coefs, dacc, bents, adv, other, gw, wave,
    four, turned, send, recv, rs_src, rs_recv, ag_src, ag_recv,
    load_sem, send_sem, recv_sem, psend_sem, precv_sem, rs_sem, ag_sem,
):
    me, mine = lax.axis_index("tile"), lax.axis_index("pair")
    flat = mine * tiles + me
    count = tiles * pairs
    halves = BLOCKS // 2
    rows = levels * SIDE // BLOCKS
    width = 256
    buddy = mine + 1 - 2 * lax.rem(mine, 2)

    loads = [
        pltpu.make_async_copy(src, dst, load_sem.at[i])
        for i, (src, dst) in enumerate(((leg_hbm, leg), (pert_hbm, pert), (target_hbm, target)))
    ]
    for load in loads:
        load.start()

    barrier = pltpu.get_barrier_semaphore()

    def greet(step, _):
        to = lax.rem(flat + step, count)
        pl.semaphore_signal(
            barrier, inc=1,
            device_id={"tile": lax.rem(to, tiles), "pair": to // tiles}, device_id_type=MESH,
        )
        return 0

    lax.fori_loop(1, count, greet, 0)

    def all_to_all(slot):
        def one(step, _):
            to = lax.rem(me + step, tiles)
            pltpu.make_async_remote_copy(
                src_ref=send.at[slot, to], dst_ref=recv.at[slot, me],
                send_sem=send_sem.at[slot], recv_sem=recv_sem.at[slot],
                device_id={"tile": to}, device_id_type=MESH,
            ).start()
            return 0

        lax.fori_loop(1, tiles, one, 0)
        pltpu.make_async_copy(send.at[slot, me], recv.at[slot, me], recv_sem.at[slot]).start()

    def arrived(slot):
        pltpu.make_async_copy(recv.at[slot], recv.at[slot], recv_sem.at[slot]).wait()

    def analyse(slot, grid):
        four[...] = lax.dot_general(
            table[...], grid, (((1,), (1,)), ((), ())), preferred_element_type=F32
        )
        for at in range(0, 32, 8):
            parts = exchanged([four[c * 32 + at : c * 32 + at + 8, :] for c in range(16)])
            for g in range(16):
                turned[pl.ds(g * STEP_OUT + at, 8), :] = parts[g]
        for row in range(32):
            send[slot, row // 2, row % 2] = turned[pl.ds(row, 16, stride=STEP_OUT), :].astype(BF16)

    def synthesise(slot):
        for row in range(32):
            turned[pl.ds(row * STEP_IN, 16), :] = recv[slot, row // 2, row % 2].astype(F32)
        for at in range(0, 32, 8):
            parts = exchanged(
                [turned[pl.ds(at * STEP_IN + g, 8, stride=STEP_IN), :] for g in range(16)]
            )
            for c in range(16):
                four[c * 32 + at : c * 32 + at + 8, :] = parts[c]
        wave[...] = lax.dot_general(
            four[...].astype(BF16), table[...], (((0,), (0,)), ((), ())),
            preferred_element_type=F32,
        )

    lane_m = lax.rem(lax.broadcasted_iota(jnp.int32, (SIDE * 16, width), 1), 16) // 2

    def spread(value):
        for m in range(8):
            rhs[pl.ds(m * 256, 256), :] = jnp.where(lane_m == m, value, 0.0).astype(BF16)

    def spectral(half, phase, backward):
        first = phase * BLOCKS + 2 * half
        for hi in range(2):
            held = [
                recv[first + b, :, hi].reshape(SIDE * SIDE, 128).astype(F32) for b in range(2)
            ]
            spread(jnp.concatenate(held, axis=1))
            coef = jnp.dot(mk_n[hi], rhs[...], preferred_element_type=F32)
            if backward:
                product = coefs[half, hi] * coef
                dacc[half] = product if hi == 0 else dacc[half] + product
            else:
                coefs[half, hi] = coef
            spread(coef * gain[half])
            back = jnp.dot(mk_g[hi], rhs[...], preferred_element_type=F32).astype(BF16)
            for b in range(2):
                send[first + BLOCKS + b, :, hi] = back[:, b * 128 : b * 128 + 128].reshape(
                    SIDE, SIDE, 128
                )

    def pick(half):
        level = lax.broadcasted_iota(jnp.int32, (levels, width), 0)
        lane = lax.broadcasted_iota(jnp.int32, (levels, width), 1)
        return (level == half * 16 + lane // 16).astype(F32)

    def exchange(ch):
        return pltpu.make_async_remote_copy(
            src_ref=adv.at[ch], dst_ref=other.at[ch],
            send_sem=psend_sem.at[ch], recv_sem=precv_sem.at[ch],
            device_id={"pair": buddy}, device_id_type=MESH,
        )

    for ch in range(BLOCKS):
        analyse(ch, state[pl.ds(ch * rows, rows), :])
        if ch == 0:
            pl.semaphore_wait(barrier, count - 1)
        all_to_all(ch)

    loads[0].wait()
    for i in range(16):
        degree = lax.broadcasted_iota(jnp.int32, (256, 256), 0)
        own = jnp.where(degree >= me * SIDE + i, leg[i].astype(F32), 0.0)
        at = pl.ds((i % 8) * 256, 256)
        mk_n[i // 8, :, at] = own.astype(BF16)
        mk_g[i // 8, :, at] = own.T.astype(BF16)
    for ch in range(halves):
        gain[ch] = lax.dot_general(
            damp[...], pick(ch), (((0,), (0,)), ((), ())),
            precision=lax.Precision.HIGHEST, preferred_element_type=F32,
        )
    loads[1].wait()
    loads[2].wait()

    def through(phase, backward):
        for half in range(halves):
            for b in range(2):
                arrived(phase * BLOCKS + 2 * half + b)
            spectral(half, phase, backward)
            for b in range(2):
                all_to_all((phase + 1) * BLOCKS + 2 * half + b)

    through(0, False)

    def forward(ch):
        arrived(BLOCKS + ch)
        synthesise(BLOCKS + ch)

        def advance(step, _):
            at = pl.ds(pl.multiple_of(step * 16, 16), 16)
            all_at = pl.ds(pl.multiple_of(ch * rows + step * 16, 16), 16)
            bent = jnp.tanh(wave[at, :])
            bents[all_at, :] = bent
            adv[ch, at, :] = (
                state[all_at, :].astype(F32) + bent + pert[all_at, :].astype(F32)
            ).astype(BF16)
            return 0

        lax.fori_loop(0, rows // 16, advance, 0)
        exchange(ch).start()

    def reverse(ch):
        exchange(ch).wait_recv()

        def gradient(step, _):
            at = pl.ds(pl.multiple_of(step * 16, 16), 16)
            all_at = pl.ds(pl.multiple_of(ch * rows + step * 16, 16), 16)
            own = adv[ch, at, :].astype(F32)
            miss = own - target[all_at, :].astype(F32)
            apart = own - other[ch, at, :].astype(F32)
            grad_adv = 0.5 * miss * lax.rsqrt(miss * miss + 1.0) - 0.25 * apart * lax.rsqrt(
                apart * apart + 1.0
            )
            bent = bents[all_at, :]
            out[all_at, :] = grad_adv
            gw[at, :] = (grad_adv * (1.0 - bent * bent)).astype(BF16)
            return 0

        lax.fori_loop(0, rows // 16, gradient, 0)
        analyse(2 * BLOCKS + ch, gw[...])
        all_to_all(2 * BLOCKS + ch)

    forward(0)
    for ch in range(1, BLOCKS):
        forward(ch)
        reverse(ch - 1)
    reverse(BLOCKS - 1)

    through(2, True)

    partial = sum(
        lax.dot_general(
            pick(ch), dacc[ch], (((1,), (1,)), ((), ())),
            precision=lax.Precision.HIGHEST, preferred_element_type=F32,
        )
        for ch in range(halves)
    )
    owners = levels // 8 * 2
    for k in range(owners):
        rs_src[k] = partial[k // 2 * 8 : k // 2 * 8 + 8, k % 2 * 128 : k % 2 * 128 + 128]

    def rs_copy(k):
        return pltpu.make_async_remote_copy(
            src_ref=rs_src.at[k], dst_ref=rs_recv.at[flat],
            send_sem=rs_sem.at[1 + k], recv_sem=rs_sem.at[0],
            device_id={"tile": 2 * k, "pair": k % pairs}, device_id_type=MESH,
        )

    for k in range(owners):
        is_owner = flat == (k % pairs) * tiles + 2 * k

        @pl.when(jnp.logical_not(is_owner))
        def _():
            rs_copy(k).start()

        @pl.when(is_owner)
        def _():
            pltpu.make_async_copy(rs_src.at[k], rs_recv.at[flat], rs_sem.at[0]).start()

    block = me // 2
    owns = jnp.logical_and(lax.rem(me, 2) == 0, lax.rem(block, pairs) == mine)

    def finish(ch):
        arrived(3 * BLOCKS + ch)
        synthesise(3 * BLOCKS + ch)
        at = pl.ds(ch * rows, rows)
        out[at, :] = out[at, :] + wave[...]

    finish(0)

    @pl.when(owns)
    def _():
        pltpu.make_async_copy(rs_recv, rs_recv, rs_sem.at[0]).wait()
        ag_src[...] = jnp.sum(rs_recv[...], axis=0)

        def one(step, _):
            to = lax.rem(flat + step, count)
            pltpu.make_async_remote_copy(
                src_ref=ag_src, dst_ref=ag_recv.at[block],
                send_sem=ag_sem.at[1], recv_sem=ag_sem.at[0],
                device_id={"tile": lax.rem(to, tiles), "pair": to // tiles}, device_id_type=MESH,
            ).start()
            return 0

        lax.fori_loop(1, count, one, 0)
        pltpu.make_async_copy(ag_src, ag_recv.at[block], ag_sem.at[0]).start()

    for ch in range(1, BLOCKS):
        finish(ch)

    pltpu.make_async_copy(ag_recv, ag_recv, ag_sem.at[0]).wait()
    for k in range(owners):
        total[k // 2 * 8 : k // 2 * 8 + 8, k % 2 * 128 : k % 2 * 128 + 128] = ag_recv[k] * (
            (pairs * tiles * SIDE) ** (-0.5)
        )

    for slot in range(4 * BLOCKS):
        gone = send.at[slot, pl.ds(0, tiles - 1)]
        pltpu.make_async_copy(gone, gone, send_sem.at[slot]).wait()
    for ch in range(BLOCKS):
        exchange(ch).wait_send()
    for k in range(owners):
        @pl.when(flat != (k % pairs) * tiles + 2 * k)
        def _():
            rs_copy(k).wait_send()

    @pl.when(owns)
    def _():
        gone = rs_recv.at[pl.ds(0, count - 1)]
        pltpu.make_async_copy(gone, gone, ag_sem.at[1]).wait()


def fused(tiles, pairs, state, target, perturbation, legendre, damp):
    members, levels, lats, lons = state.shape
    rows = levels * lats
    part = rows // BLOCKS
    width = 256
    flatten = lambda x: x.reshape(rows, lons)
    dma = pltpu.SemaphoreType.DMA
    grads, total = pl.pallas_call(
        functools.partial(kernel, tiles, pairs, levels),
        out_shape=(
            jax.ShapeDtypeStruct((rows, lons), F32),
            jax.ShapeDtypeStruct(damp.shape, F32),
        ),
        in_specs=[pl.BlockSpec(memory_space=pltpu.VMEM)] * 3
        + [pl.BlockSpec(memory_space=pl.ANY)] * 3,
        out_specs=(pl.BlockSpec(memory_space=pltpu.VMEM),) * 2,
        scratch_shapes=[
            pltpu.VMEM((rows, lons), BF16),
            pltpu.VMEM((rows, lons), BF16),
            pltpu.VMEM(legendre.shape, BF16),
            pltpu.VMEM((2, 256, 2048), BF16),
            pltpu.VMEM((2, 256, 2048), BF16),
            pltpu.VMEM((2048, width), BF16),
            pltpu.VMEM((2, 256, width), F32),
            pltpu.VMEM((2, 2, 256, width), F32),
            pltpu.VMEM((2, 256, width), F32),
            pltpu.VMEM((rows, lons), F32),
            pltpu.VMEM((BLOCKS, part, lons), BF16),
            pltpu.VMEM((BLOCKS, part, lons), BF16),
            pltpu.VMEM((part, lons), BF16),
            pltpu.VMEM((part, lons), F32),
            pltpu.VMEM((512, 128), F32),
            pltpu.VMEM((32 * STEP_IN, 128), F32),
            pltpu.VMEM((4 * BLOCKS, tiles, 2, SIDE, 128), BF16),
            pltpu.VMEM((4 * BLOCKS, tiles, 2, SIDE, 128), BF16),
            pltpu.VMEM((8, 8, 128), F32),
            pltpu.VMEM((tiles * pairs, 8, 128), F32),
            pltpu.VMEM((8, 128), F32),
            pltpu.VMEM((8, 8, 128), F32),
            dma((3,)),
            dma((4 * BLOCKS,)),
            dma((4 * BLOCKS,)),
            dma((BLOCKS,)),
            dma((BLOCKS,)),
            dma((9,)),
            dma((2,)),
        ],
        compiler_params=pltpu.CompilerParams(
            collective_id=0, has_side_effects=True, vmem_limit_bytes=48 * 2**20
        ),
    )(
        flatten(state), jnp.asarray(table_rows(NLON, M)), damp,
        flatten(target), flatten(perturbation), legendre,
    )
    return grads.reshape(state.shape), total


def solution(mesh):
    placed = (
        P("pair", None, "tile", None),
        P("pair", None, "tile", None),
        P("pair", None, "tile", None),
        P("tile", None, None),
        P(),
    )
    tiles, pairs = mesh.shape["tile"], mesh.shape["pair"]

    def local(state, target, perturbation, legendre, damp):
        held = (state.shape, legendre.shape, damp.shape)
        small = ((1, 32, SIDE, NLON), (SIDE, 256, 256), (32, 256))
        if tiles == SIDE and pairs == 2 and held == small:
            return fused(tiles, pairs, state, target, perturbation, legendre, damp)
        return body(state, target, perturbation, legendre, damp)

    return jax.shard_map(
        local,
        mesh=mesh,
        in_specs=placed,
        out_specs=(P("pair", None, "tile", None), P()),
        check_vma=False,
    )
```

```python
import functools
import math

import jax
import jax.numpy as jnp
import ml_dtypes
import numpy as np
from jax import lax
from jax.experimental import pallas as pl
from jax.experimental.pallas import tpu as pltpu
from jax.sharding import PartitionSpec as P

NLON = 512
M = 256


def swapped(value, axis, distance):
    mask = 2**distance
    pairs = [(source, source ^ mask) for source in range(lax.axis_size(axis))]
    return lax.ppermute(value, axis, pairs)


def fourier_table(length, waves):
    points = jnp.arange(length, dtype=jnp.int32)
    orders = jnp.arange(waves, dtype=jnp.int32)
    phase = points[:, None] * orders[None, :] % length
    angle = phase.astype(jnp.float32) * (2.0 * math.pi / length)
    stacked = jnp.stack([jnp.cos(angle), -jnp.sin(angle)], axis=1)
    return (stacked * length ** (-0.5)).astype(jnp.bfloat16)


def body(state, target, perturbation, legendre, damp):
    table = fourier_table(NLON, M)
    waves_dev = legendre.shape[0]
    first = lax.axis_index("tile") * waves_dev
    wave_ids = first + jnp.arange(waves_dev, dtype=jnp.int32)
    degree = jnp.arange(legendre.shape[1], dtype=jnp.int32)
    masked = jnp.where(
        degree[None, :, None] >= wave_ids[:, None, None], legendre, jnp.zeros_like(legendre)
    )
    gain = damp[None, :, None, None, :]

    def analyse(grid):
        return jnp.einsum(
            "blgj,jrm->blrmg", grid, table, preferred_element_type=jnp.float32
        ).astype(jnp.bfloat16)

    def synthesise(spec):
        return jnp.einsum("blrmg,jrm->blgj", spec, table, preferred_element_type=jnp.float32)

    def spectral_pass(piece, sender):
        coef = jnp.einsum("blrmg,mng->blrmn", piece, masked, preferred_element_type=jnp.float32)
        filtered = (coef * gain).astype(jnp.bfloat16)
        back = jnp.einsum(
            "blrmn,mng->blrmg", filtered, masked, preferred_element_type=jnp.float32
        ).astype(jnp.bfloat16)
        return (sender(back), coef)

    def to_grid(back):
        return lax.all_to_all(back, "tile", split_axis=4, concat_axis=3, tiled=True)

    def spectral(grid_coef):
        spec = lax.all_to_all(grid_coef, "tile", split_axis=3, concat_axis=4, tiled=True)
        return spectral_pass(spec, to_grid)

    back_grid, coef = spectral(analyse(state))
    bent = jnp.tanh(synthesise(back_grid))
    advanced = (state.astype(jnp.float32) + bent + perturbation.astype(jnp.float32)).astype(
        jnp.bfloat16
    )
    partner = swapped(advanced, "pair", 0)
    mine = advanced.astype(jnp.float32)
    miss = mine - target.astype(jnp.float32)
    spread = mine - partner.astype(jnp.float32)
    grad_adv = 0.5 * miss * lax.rsqrt(miss * miss + 1.0) - 0.25 * spread * lax.rsqrt(
        spread * spread + 1.0
    )
    grad_wave = (grad_adv * (1.0 - bent * bent)).astype(jnp.bfloat16)
    grad_fourier, grad_coef = spectral(analyse(grad_wave))
    grad_state = grad_adv + synthesise(grad_fourier)
    partial_sum = jnp.sum(coef * grad_coef, axis=(0, 2, 3))
    total = lax.psum(partial_sum, ("tile", "pair"))
    members = state.shape[0] * lax.axis_size("pair")
    return (grad_state, total * (members * M) ** (-0.5))


MESH = pl.DeviceIdType.MESH
BF16, F32 = jnp.bfloat16, jnp.float32
SIDE = 16
BLOCKS = 4
STEP_OUT, STEP_IN = 40, 24


def table_rows(length, waves):
    points = np.arange(length)
    orders = np.arange(waves)
    angle = (points[:, None] * orders[None, :] % length) * (2.0 * math.pi / length)
    both = np.stack([np.cos(angle), -np.sin(angle)], axis=0) * length ** (-0.5)
    split = both.reshape(2, length, waves // SIDE, 2, 8)
    return split.transpose(4, 0, 2, 3, 1).reshape(2 * waves, length).astype(ml_dtypes.bfloat16)


def exchanged(parts):
    lane = lax.broadcasted_iota(jnp.int32, parts[0].shape, 1)
    parts = list(parts)
    for bit in (1, 2, 4, 8):
        high = (lane & bit) != 0
        for i in range(16):
            if not i & bit:
                a, b = parts[i], parts[i | bit]
                parts[i] = jnp.where(high, pltpu.roll(b, bit, 1), a)
                parts[i | bit] = jnp.where(high, b, pltpu.roll(a, 128 - bit, 1))
    return parts


def kernel(
    tiles, pairs, levels,
    state_hbm, table_hbm, damp_hbm, target_hbm, pert_hbm, leg_hbm,
    out, total,
    state, table, damp, target, pert, leg, mk_n, mk_g, rhs, gain, coefs, dacc, bents, adv, other, gw, wave,
    four, turned, send, recv, rs_src, rs_recv, ag_src, ag_recv,
    load_sem, send_sem, recv_sem, psend_sem, precv_sem, rs_sem, ag_sem,
):
    me, mine = lax.axis_index("tile"), lax.axis_index("pair")
    flat = mine * tiles + me
    count = tiles * pairs
    halves = BLOCKS // 2
    rows = levels * SIDE // BLOCKS
    width = 256
    buddy = mine + 1 - 2 * lax.rem(mine, 2)

    pairs_of_refs = (
        (table_hbm, table), (state_hbm, state), (leg_hbm, leg),
        (damp_hbm, damp), (pert_hbm, pert), (target_hbm, target),
    )
    loads = [
        pltpu.make_async_copy(src, dst, load_sem.at[i])
        for i, (src, dst) in enumerate(pairs_of_refs)
    ]
    loads[0].start()
    loads[1].start()

    barrier = pltpu.get_barrier_semaphore()

    def greet(step, _):
        to = lax.rem(flat + step, count)
        pl.semaphore_signal(
            barrier, inc=1,
            device_id={"tile": lax.rem(to, tiles), "pair": to // tiles}, device_id_type=MESH,
        )
        return 0

    lax.fori_loop(1, count, greet, 0)

    def all_to_all(slot):
        def one(step, _):
            to = lax.rem(me + step, tiles)
            pltpu.make_async_remote_copy(
                src_ref=send.at[slot, to], dst_ref=recv.at[slot, me],
                send_sem=send_sem.at[slot], recv_sem=recv_sem.at[slot],
                device_id={"tile": to}, device_id_type=MESH,
            ).start()
            return 0

        lax.fori_loop(1, tiles, one, 0)
        pltpu.make_async_copy(send.at[slot, me], recv.at[slot, me], recv_sem.at[slot]).start()

    def arrived(slot):
        pltpu.make_async_copy(recv.at[slot], recv.at[slot], recv_sem.at[slot]).wait()

    def analyse(slot, grid):
        four[...] = lax.dot_general(
            table[...], grid, (((1,), (1,)), ((), ())), preferred_element_type=F32
        )
        for at in range(0, 32, 8):
            parts = exchanged([four[c * 32 + at : c * 32 + at + 8, :] for c in range(16)])
            for g in range(16):
                turned[pl.ds(g * STEP_OUT + at, 8), :] = parts[g]
        for row in range(32):
            send[slot, row // 2, row % 2] = turned[pl.ds(row, 16, stride=STEP_OUT), :].astype(BF16)

    def synthesise(slot):
        for row in range(32):
            turned[pl.ds(row * STEP_IN, 16), :] = recv[slot, row // 2, row % 2].astype(F32)
        for at in range(0, 32, 8):
            parts = exchanged(
                [turned[pl.ds(at * STEP_IN + g, 8, stride=STEP_IN), :] for g in range(16)]
            )
            for c in range(16):
                four[c * 32 + at : c * 32 + at + 8, :] = parts[c]
        wave[...] = lax.dot_general(
            four[...].astype(BF16), table[...], (((0,), (0,)), ((), ())),
            preferred_element_type=F32,
        )

    lane_m = lax.rem(lax.broadcasted_iota(jnp.int32, (SIDE * 16, width), 1), 16) // 2

    def spread(value):
        for m in range(8):
            rhs[pl.ds(m * 256, 256), :] = jnp.where(lane_m == m, value, 0.0).astype(BF16)

    def spectral(half, phase, backward):
        first = phase * BLOCKS + 2 * half
        for hi in range(2):
            held = [
                recv[first + b, :, hi].reshape(SIDE * SIDE, 128).astype(F32) for b in range(2)
            ]
            spread(jnp.concatenate(held, axis=1))
            coef = jnp.dot(mk_n[hi], rhs[...], preferred_element_type=F32)
            if backward:
                product = coefs[half, hi] * coef
                dacc[half] = product if hi == 0 else dacc[half] + product
            else:
                coefs[half, hi] = coef
            spread(coef * gain[half])
            back = jnp.dot(mk_g[hi], rhs[...], preferred_element_type=F32).astype(BF16)
            for b in range(2):
                send[first + BLOCKS + b, :, hi] = back[:, b * 128 : b * 128 + 128].reshape(
                    SIDE, SIDE, 128
                )

    def pick(half):
        level = lax.broadcasted_iota(jnp.int32, (levels, width), 0)
        lane = lax.broadcasted_iota(jnp.int32, (levels, width), 1)
        return (level == half * 16 + lane // 16).astype(F32)

    def exchange(ch):
        return pltpu.make_async_remote_copy(
            src_ref=adv.at[ch], dst_ref=other.at[ch],
            send_sem=psend_sem.at[ch], recv_sem=precv_sem.at[ch],
            device_id={"pair": buddy}, device_id_type=MESH,
        )

    for load in loads[2:]:
        load.start()

    loads[0].wait()
    loads[1].wait()
    for ch in range(BLOCKS):
        analyse(ch, state[pl.ds(ch * rows, rows), :])
        if ch == 0:
            pl.semaphore_wait(barrier, count - 1)
        all_to_all(ch)

    loads[2].wait()
    for i in range(16):
        degree = lax.broadcasted_iota(jnp.int32, (256, 256), 0)
        own = jnp.where(degree >= me * SIDE + i, leg[i].astype(F32), 0.0)
        at = pl.ds((i % 8) * 256, 256)
        mk_n[i // 8, :, at] = own.astype(BF16)
        mk_g[i // 8, :, at] = own.T.astype(BF16)
    loads[3].wait()
    for ch in range(halves):
        gain[ch] = lax.dot_general(
            damp[...], pick(ch), (((0,), (0,)), ((), ())),
            precision=lax.Precision.HIGHEST, preferred_element_type=F32,
        )
    loads[4].wait()
    loads[5].wait()

    owners = levels // 8 * 2
    block = me // 2
    owns = jnp.logical_and(lax.rem(me, 2) == 0, lax.rem(block, pairs) == mine)

    def rs_copy(k):
        return pltpu.make_async_remote_copy(
            src_ref=rs_src.at[k], dst_ref=rs_recv.at[flat],
            send_sem=rs_sem.at[1 + k], recv_sem=rs_sem.at[0],
            device_id={"tile": 2 * k, "pair": k % pairs}, device_id_type=MESH,
        )

    def to_owners(half):
        partial = lax.dot_general(
            pick(half)[half * 16 : half * 16 + 16], dacc[half], (((1,), (1,)), ((), ())),
            precision=lax.Precision.HIGHEST, preferred_element_type=F32,
        )
        for k in range(half * 4, half * 4 + 4):
            row, col = k % 4 // 2 * 8, k % 2 * 128
            rs_src[k] = partial[row : row + 8, col : col + 128]
            is_owner = flat == (k % pairs) * tiles + 2 * k

            @pl.when(jnp.logical_not(is_owner))
            def _():
                rs_copy(k).start()

            @pl.when(is_owner)
            def _():
                pltpu.make_async_copy(rs_src.at[k], rs_recv.at[flat], rs_sem.at[0]).start()

    def from_owners(half):
        @pl.when(jnp.logical_and(owns, block // 4 == half))
        def _():
            pltpu.make_async_copy(rs_recv, rs_recv, rs_sem.at[0]).wait()
            ag_src[...] = jnp.sum(rs_recv[...], axis=0)

            def one(step, _):
                to = lax.rem(flat + step, count)
                pltpu.make_async_remote_copy(
                    src_ref=ag_src, dst_ref=ag_recv.at[block],
                    send_sem=ag_sem.at[1], recv_sem=ag_sem.at[0],
                    device_id={"tile": lax.rem(to, tiles), "pair": to // tiles},
                    device_id_type=MESH,
                ).start()
                return 0

            lax.fori_loop(1, count, one, 0)
            pltpu.make_async_copy(ag_src, ag_recv.at[block], ag_sem.at[0]).start()

    def through(phase, backward):
        for half in range(halves):
            for b in range(2):
                arrived(phase * BLOCKS + 2 * half + b)
            spectral(half, phase, backward)
            if backward:
                to_owners(half)
            for b in range(2):
                all_to_all((phase + 1) * BLOCKS + 2 * half + b)

    through(0, False)

    def forward(ch):
        arrived(BLOCKS + ch)
        synthesise(BLOCKS + ch)

        def advance(step, _):
            at = pl.ds(pl.multiple_of(step * 16, 16), 16)
            all_at = pl.ds(pl.multiple_of(ch * rows + step * 16, 16), 16)
            bent = jnp.tanh(wave[at, :])
            bents[all_at, :] = bent
            adv[ch, at, :] = (
                state[all_at, :].astype(F32) + bent + pert[all_at, :].astype(F32)
            ).astype(BF16)
            return 0

        lax.fori_loop(0, rows // 16, advance, 0)
        exchange(ch).start()

    def reverse(ch):
        exchange(ch).wait_recv()

        def gradient(step, _):
            at = pl.ds(pl.multiple_of(step * 16, 16), 16)
            all_at = pl.ds(pl.multiple_of(ch * rows + step * 16, 16), 16)
            own = adv[ch, at, :].astype(F32)
            miss = own - target[all_at, :].astype(F32)
            apart = own - other[ch, at, :].astype(F32)
            grad_adv = 0.5 * miss * lax.rsqrt(miss * miss + 1.0) - 0.25 * apart * lax.rsqrt(
                apart * apart + 1.0
            )
            bent = bents[all_at, :]
            out[all_at, :] = grad_adv
            gw[at, :] = (grad_adv * (1.0 - bent * bent)).astype(BF16)
            return 0

        lax.fori_loop(0, rows // 16, gradient, 0)
        analyse(2 * BLOCKS + ch, gw[...])
        all_to_all(2 * BLOCKS + ch)

    forward(0)
    for ch in range(1, BLOCKS):
        forward(ch)
        reverse(ch - 1)
    reverse(BLOCKS - 1)

    through(2, True)

    def finish(ch):
        arrived(3 * BLOCKS + ch)
        synthesise(3 * BLOCKS + ch)
        at = pl.ds(ch * rows, rows)
        out[at, :] = out[at, :] + wave[...]

    from_owners(0)
    finish(0)
    finish(1)
    from_owners(1)
    for ch in range(2, BLOCKS):
        finish(ch)

    pltpu.make_async_copy(ag_recv, ag_recv, ag_sem.at[0]).wait()
    for k in range(owners):
        total[k // 2 * 8 : k // 2 * 8 + 8, k % 2 * 128 : k % 2 * 128 + 128] = ag_recv[k] * (
            (pairs * tiles * SIDE) ** (-0.5)
        )

    for slot in range(4 * BLOCKS):
        gone = send.at[slot, pl.ds(0, tiles - 1)]
        pltpu.make_async_copy(gone, gone, send_sem.at[slot]).wait()
    for ch in range(BLOCKS):
        exchange(ch).wait_send()
    for k in range(owners):
        @pl.when(flat != (k % pairs) * tiles + 2 * k)
        def _():
            rs_copy(k).wait_send()

    @pl.when(owns)
    def _():
        gone = rs_recv.at[pl.ds(0, count - 1)]
        pltpu.make_async_copy(gone, gone, ag_sem.at[1]).wait()


def fused(tiles, pairs, state, target, perturbation, legendre, damp):
    members, levels, lats, lons = state.shape
    rows = levels * lats
    part = rows // BLOCKS
    width = 256
    flatten = lambda x: x.reshape(rows, lons)
    dma = pltpu.SemaphoreType.DMA
    grads, total = pl.pallas_call(
        functools.partial(kernel, tiles, pairs, levels),
        out_shape=(
            jax.ShapeDtypeStruct((rows, lons), F32),
            jax.ShapeDtypeStruct(damp.shape, F32),
        ),
        in_specs=[pl.BlockSpec(memory_space=pltpu.HBM)] * 6,
        out_specs=(pl.BlockSpec(memory_space=pltpu.VMEM),) * 2,
        scratch_shapes=[
            pltpu.VMEM((rows, lons), BF16),
            pltpu.VMEM((2 * M, NLON), BF16),
            pltpu.VMEM(damp.shape, F32),
            pltpu.VMEM((rows, lons), BF16),
            pltpu.VMEM((rows, lons), BF16),
            pltpu.VMEM(legendre.shape, BF16),
            pltpu.VMEM((2, 256, 2048), BF16),
            pltpu.VMEM((2, 256, 2048), BF16),
            pltpu.VMEM((2048, width), BF16),
            pltpu.VMEM((2, 256, width), F32),
            pltpu.VMEM((2, 2, 256, width), F32),
            pltpu.VMEM((2, 256, width), F32),
            pltpu.VMEM((rows, lons), F32),
            pltpu.VMEM((BLOCKS, part, lons), BF16),
            pltpu.VMEM((BLOCKS, part, lons), BF16),
            pltpu.VMEM((part, lons), BF16),
            pltpu.VMEM((part, lons), F32),
            pltpu.VMEM((512, 128), F32),
            pltpu.VMEM((32 * STEP_IN, 128), F32),
            pltpu.VMEM((4 * BLOCKS, tiles, 2, SIDE, 128), BF16),
            pltpu.VMEM((4 * BLOCKS, tiles, 2, SIDE, 128), BF16),
            pltpu.VMEM((8, 8, 128), F32),
            pltpu.VMEM((tiles * pairs, 8, 128), F32),
            pltpu.VMEM((8, 128), F32),
            pltpu.VMEM((8, 8, 128), F32),
            dma((6,)),
            dma((4 * BLOCKS,)),
            dma((4 * BLOCKS,)),
            dma((BLOCKS,)),
            dma((BLOCKS,)),
            dma((9,)),
            dma((2,)),
        ],
        compiler_params=pltpu.CompilerParams(
            collective_id=0, has_side_effects=True, vmem_limit_bytes=48 * 2**20
        ),
    )(
        flatten(state), jnp.asarray(table_rows(NLON, M)), damp,
        flatten(target), flatten(perturbation), legendre,
    )
    return grads.reshape(state.shape), total


def solution(mesh):
    placed = (
        P("pair", None, "tile", None),
        P("pair", None, "tile", None),
        P("pair", None, "tile", None),
        P("tile", None, None),
        P(),
    )
    tiles, pairs = mesh.shape["tile"], mesh.shape["pair"]

    def local(state, target, perturbation, legendre, damp):
        held = (state.shape, legendre.shape, damp.shape)
        small = ((1, 32, SIDE, NLON), (SIDE, 256, 256), (32, 256))
        if tiles == SIDE and pairs == 2 and held == small:
            return fused(tiles, pairs, state, target, perturbation, legendre, damp)
        return body(state, target, perturbation, legendre, damp)

    return jax.shard_map(
        local,
        mesh=mesh,
        in_specs=placed,
        out_specs=(P("pair", None, "tile", None), P()),
        check_vma=False,
    )
```

```python
import functools
import math

import jax
import jax.numpy as jnp
import ml_dtypes
import numpy as np
from jax import lax
from jax.experimental import pallas as pl
from jax.experimental.pallas import tpu as pltpu
from jax.sharding import PartitionSpec as P

NLON = 512
M = 256


def swapped(value, axis, distance):
    mask = 2**distance
    pairs = [(source, source ^ mask) for source in range(lax.axis_size(axis))]
    return lax.ppermute(value, axis, pairs)


def fourier_table(length, waves):
    points = jnp.arange(length, dtype=jnp.int32)
    orders = jnp.arange(waves, dtype=jnp.int32)
    phase = points[:, None] * orders[None, :] % length
    angle = phase.astype(jnp.float32) * (2.0 * math.pi / length)
    stacked = jnp.stack([jnp.cos(angle), -jnp.sin(angle)], axis=1)
    return (stacked * length ** (-0.5)).astype(jnp.bfloat16)


def body(state, target, perturbation, legendre, damp):
    table = fourier_table(NLON, M)
    waves_dev = legendre.shape[0]
    first = lax.axis_index("tile") * waves_dev
    wave_ids = first + jnp.arange(waves_dev, dtype=jnp.int32)
    degree = jnp.arange(legendre.shape[1], dtype=jnp.int32)
    masked = jnp.where(
        degree[None, :, None] >= wave_ids[:, None, None], legendre, jnp.zeros_like(legendre)
    )
    gain = damp[None, :, None, None, :]

    def analyse(grid):
        return jnp.einsum(
            "blgj,jrm->blrmg", grid, table, preferred_element_type=jnp.float32
        ).astype(jnp.bfloat16)

    def synthesise(spec):
        return jnp.einsum("blrmg,jrm->blgj", spec, table, preferred_element_type=jnp.float32)

    def spectral_pass(piece, sender):
        coef = jnp.einsum("blrmg,mng->blrmn", piece, masked, preferred_element_type=jnp.float32)
        filtered = (coef * gain).astype(jnp.bfloat16)
        back = jnp.einsum(
            "blrmn,mng->blrmg", filtered, masked, preferred_element_type=jnp.float32
        ).astype(jnp.bfloat16)
        return (sender(back), coef)

    def to_grid(back):
        return lax.all_to_all(back, "tile", split_axis=4, concat_axis=3, tiled=True)

    def spectral(grid_coef):
        spec = lax.all_to_all(grid_coef, "tile", split_axis=3, concat_axis=4, tiled=True)
        return spectral_pass(spec, to_grid)

    back_grid, coef = spectral(analyse(state))
    bent = jnp.tanh(synthesise(back_grid))
    advanced = (state.astype(jnp.float32) + bent + perturbation.astype(jnp.float32)).astype(
        jnp.bfloat16
    )
    partner = swapped(advanced, "pair", 0)
    mine = advanced.astype(jnp.float32)
    miss = mine - target.astype(jnp.float32)
    spread = mine - partner.astype(jnp.float32)
    grad_adv = 0.5 * miss * lax.rsqrt(miss * miss + 1.0) - 0.25 * spread * lax.rsqrt(
        spread * spread + 1.0
    )
    grad_wave = (grad_adv * (1.0 - bent * bent)).astype(jnp.bfloat16)
    grad_fourier, grad_coef = spectral(analyse(grad_wave))
    grad_state = grad_adv + synthesise(grad_fourier)
    partial_sum = jnp.sum(coef * grad_coef, axis=(0, 2, 3))
    total = lax.psum(partial_sum, ("tile", "pair"))
    members = state.shape[0] * lax.axis_size("pair")
    return (grad_state, total * (members * M) ** (-0.5))


MESH = pl.DeviceIdType.MESH
BF16, F32 = jnp.bfloat16, jnp.float32
SIDE = 16
BLOCKS = 4
STEP_OUT, STEP_IN = 40, 24


def table_rows(length, waves):
    points = np.arange(length)
    orders = np.arange(waves)
    angle = (points[:, None] * orders[None, :] % length) * (2.0 * math.pi / length)
    both = np.stack([np.cos(angle), -np.sin(angle)], axis=0) * length ** (-0.5)
    split = both.reshape(2, length, waves // SIDE, 2, 8)
    return split.transpose(4, 0, 2, 3, 1).reshape(2 * waves, length).astype(ml_dtypes.bfloat16)


def exchanged(parts):
    lane = lax.broadcasted_iota(jnp.int32, parts[0].shape, 1)
    parts = list(parts)
    for bit in (1, 2, 4, 8):
        high = (lane & bit) != 0
        for i in range(16):
            if not i & bit:
                a, b = parts[i], parts[i | bit]
                parts[i] = jnp.where(high, pltpu.roll(b, bit, 1), a)
                parts[i | bit] = jnp.where(high, b, pltpu.roll(a, 128 - bit, 1))
    return parts


def kernel(
    tiles, pairs, levels,
    state_hbm, table_hbm, damp_hbm, target_hbm, pert_hbm, leg_hbm,
    out_hbm, total,
    out, state, table, damp, target, pert, leg, mk_n, mk_g, rhs, gain, coefs, dacc, bents, adv, other, gw, wave,
    four, turned, send, recv, rs_src, rs_recv, ag_src, ag_recv,
    load_sem, store_sem, send_sem, recv_sem, psend_sem, precv_sem, rs_sem, ag_sem,
):
    me, mine = lax.axis_index("tile"), lax.axis_index("pair")
    flat = mine * tiles + me
    count = tiles * pairs
    halves = BLOCKS // 2
    rows = levels * SIDE // BLOCKS
    width = 256
    buddy = mine + 1 - 2 * lax.rem(mine, 2)

    pairs_of_refs = (
        (table_hbm, table), (state_hbm, state), (leg_hbm, leg),
        (damp_hbm, damp), (pert_hbm, pert), (target_hbm, target),
    )
    loads = [
        pltpu.make_async_copy(src, dst, load_sem.at[i])
        for i, (src, dst) in enumerate(pairs_of_refs)
    ]
    loads[0].start()
    loads[1].start()

    barrier = pltpu.get_barrier_semaphore()

    def greet(step, _):
        to = lax.rem(flat + step, count)
        pl.semaphore_signal(
            barrier, inc=1,
            device_id={"tile": lax.rem(to, tiles), "pair": to // tiles}, device_id_type=MESH,
        )
        return 0

    lax.fori_loop(1, count, greet, 0)

    def all_to_all(slot):
        def one(step, _):
            to = lax.rem(me + step, tiles)
            pltpu.make_async_remote_copy(
                src_ref=send.at[slot, to], dst_ref=recv.at[slot, me],
                send_sem=send_sem.at[slot], recv_sem=recv_sem.at[slot],
                device_id={"tile": to}, device_id_type=MESH,
            ).start()
            return 0

        lax.fori_loop(1, tiles, one, 0)
        pltpu.make_async_copy(send.at[slot, me], recv.at[slot, me], recv_sem.at[slot]).start()

    def arrived(slot):
        pltpu.make_async_copy(recv.at[slot], recv.at[slot], recv_sem.at[slot]).wait()

    def analyse(slot, grid):
        four[...] = lax.dot_general(
            table[...], grid, (((1,), (1,)), ((), ())), preferred_element_type=F32
        )
        for at in range(0, 32, 8):
            parts = exchanged([four[c * 32 + at : c * 32 + at + 8, :] for c in range(16)])
            for g in range(16):
                turned[pl.ds(g * STEP_OUT + at, 8), :] = parts[g]
        for row in range(32):
            send[slot, row // 2, row % 2] = turned[pl.ds(row, 16, stride=STEP_OUT), :].astype(BF16)

    def synthesise(slot):
        for row in range(32):
            turned[pl.ds(row * STEP_IN, 16), :] = recv[slot, row // 2, row % 2].astype(F32)
        for at in range(0, 32, 8):
            parts = exchanged(
                [turned[pl.ds(at * STEP_IN + g, 8, stride=STEP_IN), :] for g in range(16)]
            )
            for c in range(16):
                four[c * 32 + at : c * 32 + at + 8, :] = parts[c]
        wave[...] = lax.dot_general(
            four[...].astype(BF16), table[...], (((0,), (0,)), ((), ())),
            preferred_element_type=F32,
        )

    lane_m = lax.rem(lax.broadcasted_iota(jnp.int32, (SIDE * 16, width), 1), 16) // 2

    def spread(value):
        for m in range(8):
            rhs[pl.ds(m * 256, 256), :] = jnp.where(lane_m == m, value, 0.0).astype(BF16)

    def spectral(half, phase, backward):
        first = phase * BLOCKS + 2 * half
        for hi in range(2):
            held = [
                recv[first + b, :, hi].reshape(SIDE * SIDE, 128).astype(F32) for b in range(2)
            ]
            spread(jnp.concatenate(held, axis=1))
            coef = jnp.dot(mk_n[hi], rhs[...], preferred_element_type=F32)
            if backward:
                product = coefs[half, hi] * coef
                dacc[half] = product if hi == 0 else dacc[half] + product
            else:
                coefs[half, hi] = coef
            spread(coef * gain[half])
            back = jnp.dot(mk_g[hi], rhs[...], preferred_element_type=F32).astype(BF16)
            for b in range(2):
                send[first + BLOCKS + b, :, hi] = back[:, b * 128 : b * 128 + 128].reshape(
                    SIDE, SIDE, 128
                )

    def pick(half):
        level = lax.broadcasted_iota(jnp.int32, (levels, width), 0)
        lane = lax.broadcasted_iota(jnp.int32, (levels, width), 1)
        return (level == half * 16 + lane // 16).astype(F32)

    def exchange(ch):
        return pltpu.make_async_remote_copy(
            src_ref=adv.at[ch], dst_ref=other.at[ch],
            send_sem=psend_sem.at[ch], recv_sem=precv_sem.at[ch],
            device_id={"pair": buddy}, device_id_type=MESH,
        )

    for load in loads[2:]:
        load.start()

    loads[0].wait()
    loads[1].wait()
    for ch in range(BLOCKS):
        analyse(ch, state[pl.ds(ch * rows, rows), :])
        if ch == 0:
            pl.semaphore_wait(barrier, count - 1)
        all_to_all(ch)

    loads[2].wait()
    for i in range(16):
        degree = lax.broadcasted_iota(jnp.int32, (256, 256), 0)
        own = jnp.where(degree >= me * SIDE + i, leg[i].astype(F32), 0.0)
        at = pl.ds((i % 8) * 256, 256)
        mk_n[i // 8, :, at] = own.astype(BF16)
        mk_g[i // 8, :, at] = own.T.astype(BF16)
    loads[3].wait()
    for ch in range(halves):
        gain[ch] = lax.dot_general(
            damp[...], pick(ch), (((0,), (0,)), ((), ())),
            precision=lax.Precision.HIGHEST, preferred_element_type=F32,
        )
    loads[4].wait()
    loads[5].wait()

    owners = levels // 8 * 2
    block = me // 2
    owns = jnp.logical_and(lax.rem(me, 2) == 0, lax.rem(block, pairs) == mine)

    def rs_copy(k):
        return pltpu.make_async_remote_copy(
            src_ref=rs_src.at[k], dst_ref=rs_recv.at[flat],
            send_sem=rs_sem.at[1 + k], recv_sem=rs_sem.at[0],
            device_id={"tile": 2 * k, "pair": k % pairs}, device_id_type=MESH,
        )

    def to_owners(half):
        partial = lax.dot_general(
            pick(half)[half * 16 : half * 16 + 16], dacc[half], (((1,), (1,)), ((), ())),
            precision=lax.Precision.HIGHEST, preferred_element_type=F32,
        )
        for k in range(half * 4, half * 4 + 4):
            row, col = k % 4 // 2 * 8, k % 2 * 128
            rs_src[k] = partial[row : row + 8, col : col + 128]
            is_owner = flat == (k % pairs) * tiles + 2 * k

            @pl.when(jnp.logical_not(is_owner))
            def _():
                rs_copy(k).start()

            @pl.when(is_owner)
            def _():
                pltpu.make_async_copy(rs_src.at[k], rs_recv.at[flat], rs_sem.at[0]).start()

    def from_owners(half):
        @pl.when(jnp.logical_and(owns, block // 4 == half))
        def _():
            pltpu.make_async_copy(rs_recv, rs_recv, rs_sem.at[0]).wait()
            ag_src[...] = jnp.sum(rs_recv[...], axis=0)

            def one(step, _):
                to = lax.rem(flat + step, count)
                pltpu.make_async_remote_copy(
                    src_ref=ag_src, dst_ref=ag_recv.at[block],
                    send_sem=ag_sem.at[1], recv_sem=ag_sem.at[0],
                    device_id={"tile": lax.rem(to, tiles), "pair": to // tiles},
                    device_id_type=MESH,
                ).start()
                return 0

            lax.fori_loop(1, count, one, 0)
            pltpu.make_async_copy(ag_src, ag_recv.at[block], ag_sem.at[0]).start()

    def through(phase, backward):
        for half in range(halves):
            for b in range(2):
                arrived(phase * BLOCKS + 2 * half + b)
            spectral(half, phase, backward)
            if backward:
                to_owners(half)
            for b in range(2):
                all_to_all((phase + 1) * BLOCKS + 2 * half + b)

    through(0, False)

    def forward(ch):
        arrived(BLOCKS + ch)
        synthesise(BLOCKS + ch)

        def advance(step, _):
            at = pl.ds(pl.multiple_of(step * 16, 16), 16)
            all_at = pl.ds(pl.multiple_of(ch * rows + step * 16, 16), 16)
            bent = jnp.tanh(wave[at, :])
            bents[all_at, :] = bent
            adv[ch, at, :] = (
                state[all_at, :].astype(F32) + bent + pert[all_at, :].astype(F32)
            ).astype(BF16)
            return 0

        lax.fori_loop(0, rows // 16, advance, 0)
        exchange(ch).start()

    def reverse(ch):
        exchange(ch).wait_recv()

        def gradient(step, _):
            at = pl.ds(pl.multiple_of(step * 16, 16), 16)
            all_at = pl.ds(pl.multiple_of(ch * rows + step * 16, 16), 16)
            own = adv[ch, at, :].astype(F32)
            miss = own - target[all_at, :].astype(F32)
            apart = own - other[ch, at, :].astype(F32)
            grad_adv = 0.5 * miss * lax.rsqrt(miss * miss + 1.0) - 0.25 * apart * lax.rsqrt(
                apart * apart + 1.0
            )
            bent = bents[all_at, :]
            out[all_at, :] = grad_adv
            gw[at, :] = (grad_adv * (1.0 - bent * bent)).astype(BF16)
            return 0

        lax.fori_loop(0, rows // 16, gradient, 0)
        analyse(2 * BLOCKS + ch, gw[...])
        all_to_all(2 * BLOCKS + ch)

    forward(0)
    for ch in range(1, BLOCKS):
        forward(ch)
        reverse(ch - 1)
    reverse(BLOCKS - 1)

    through(2, True)

    def store(ch):
        at = pl.ds(ch * rows, rows)
        return pltpu.make_async_copy(out.at[at, :], out_hbm.at[at, :], store_sem.at[ch])

    def finish(ch):
        arrived(3 * BLOCKS + ch)
        synthesise(3 * BLOCKS + ch)
        at = pl.ds(ch * rows, rows)
        out[at, :] = out[at, :] + wave[...]
        store(ch).start()

    from_owners(0)
    finish(0)
    finish(1)
    from_owners(1)
    for ch in range(2, BLOCKS):
        finish(ch)

    pltpu.make_async_copy(ag_recv, ag_recv, ag_sem.at[0]).wait()
    for k in range(owners):
        total[k // 2 * 8 : k // 2 * 8 + 8, k % 2 * 128 : k % 2 * 128 + 128] = ag_recv[k] * (
            (pairs * tiles * SIDE) ** (-0.5)
        )

    for ch in range(BLOCKS):
        store(ch).wait()

    for slot in range(4 * BLOCKS):
        gone = send.at[slot, pl.ds(0, tiles - 1)]
        pltpu.make_async_copy(gone, gone, send_sem.at[slot]).wait()
    for ch in range(BLOCKS):
        exchange(ch).wait_send()
    for k in range(owners):
        @pl.when(flat != (k % pairs) * tiles + 2 * k)
        def _():
            rs_copy(k).wait_send()

    @pl.when(owns)
    def _():
        gone = rs_recv.at[pl.ds(0, count - 1)]
        pltpu.make_async_copy(gone, gone, ag_sem.at[1]).wait()


def fused(tiles, pairs, state, target, perturbation, legendre, damp):
    members, levels, lats, lons = state.shape
    rows = levels * lats
    part = rows // BLOCKS
    width = 256
    flatten = lambda x: x.reshape(rows, lons)
    dma = pltpu.SemaphoreType.DMA
    grads, total = pl.pallas_call(
        functools.partial(kernel, tiles, pairs, levels),
        out_shape=(
            jax.ShapeDtypeStruct((rows, lons), F32),
            jax.ShapeDtypeStruct(damp.shape, F32),
        ),
        in_specs=[pl.BlockSpec(memory_space=pltpu.HBM)] * 6,
        out_specs=(
            pl.BlockSpec(memory_space=pl.ANY),
            pl.BlockSpec(memory_space=pltpu.VMEM),
        ),
        scratch_shapes=[
            pltpu.VMEM((rows, lons), F32),
            pltpu.VMEM((rows, lons), BF16),
            pltpu.VMEM((2 * M, NLON), BF16),
            pltpu.VMEM(damp.shape, F32),
            pltpu.VMEM((rows, lons), BF16),
            pltpu.VMEM((rows, lons), BF16),
            pltpu.VMEM(legendre.shape, BF16),
            pltpu.VMEM((2, 256, 2048), BF16),
            pltpu.VMEM((2, 256, 2048), BF16),
            pltpu.VMEM((2048, width), BF16),
            pltpu.VMEM((2, 256, width), F32),
            pltpu.VMEM((2, 2, 256, width), F32),
            pltpu.VMEM((2, 256, width), F32),
            pltpu.VMEM((rows, lons), F32),
            pltpu.VMEM((BLOCKS, part, lons), BF16),
            pltpu.VMEM((BLOCKS, part, lons), BF16),
            pltpu.VMEM((part, lons), BF16),
            pltpu.VMEM((part, lons), F32),
            pltpu.VMEM((512, 128), F32),
            pltpu.VMEM((32 * STEP_IN, 128), F32),
            pltpu.VMEM((4 * BLOCKS, tiles, 2, SIDE, 128), BF16),
            pltpu.VMEM((4 * BLOCKS, tiles, 2, SIDE, 128), BF16),
            pltpu.VMEM((8, 8, 128), F32),
            pltpu.VMEM((tiles * pairs, 8, 128), F32),
            pltpu.VMEM((8, 128), F32),
            pltpu.VMEM((8, 8, 128), F32),
            dma((6,)),
            dma((BLOCKS,)),
            dma((4 * BLOCKS,)),
            dma((4 * BLOCKS,)),
            dma((BLOCKS,)),
            dma((BLOCKS,)),
            dma((9,)),
            dma((2,)),
        ],
        compiler_params=pltpu.CompilerParams(
            collective_id=0, has_side_effects=True, vmem_limit_bytes=62 * 2**20
        ),
    )(
        flatten(state), jnp.asarray(table_rows(NLON, M)), damp,
        flatten(target), flatten(perturbation), legendre,
    )
    return grads.reshape(state.shape), total


def solution(mesh):
    placed = (
        P("pair", None, "tile", None),
        P("pair", None, "tile", None),
        P("pair", None, "tile", None),
        P("tile", None, None),
        P(),
    )
    tiles, pairs = mesh.shape["tile"], mesh.shape["pair"]

    def local(state, target, perturbation, legendre, damp):
        held = (state.shape, legendre.shape, damp.shape)
        small = ((1, 32, SIDE, NLON), (SIDE, 256, 256), (32, 256))
        if tiles == SIDE and pairs == 2 and held == small:
            return fused(tiles, pairs, state, target, perturbation, legendre, damp)
        return body(state, target, perturbation, legendre, damp)

    return jax.shard_map(
        local,
        mesh=mesh,
        in_specs=placed,
        out_specs=(P("pair", None, "tile", None), P()),
        check_vma=False,
    )
```
